128 devices in a mesh: region: 4 (over x_hi, core), fsdp: 4 (over z), tensor: 8 (over y, x_lo).
Axes of the slice: x: 4 (x_hi: 2, x_lo: 2; x = x_hi * 2 + x_lo), y: 4, z: 4, core: 2. Of those that a mesh axis runs over, the one named last changes fastest.
Arguments:
- gate_pre: bfloat16 [4, 2048, 14336], P('region', 'fsdp', 'tensor'), may hold values from -6 to 6
- up_pre: bfloat16 [4, 2048, 14336], P('region', 'fsdp', 'tensor'), may hold values from -6 to 6
- out_grad: bfloat16 [4, 2048, 4096], P('region', 'tensor', 'fsdp'), may hold values from -6 to 6
- weights: bfloat16 [4, 14336, 4096], P('region', 'tensor', 'fsdp'), may hold values from -6 to 6
- first_moment: bfloat16 [4, 14336, 4096], P('region', 'tensor', 'fsdp'), may hold values from -0.015625 to 0.015625
- second_moment: float32 [4, 14336, 4096], P('region', 'tensor', 'fsdp'), may hold values from 1e-06 to 1e-05
- anchor: float32 [8, 4, 448, 4096], P('tensor', 'region', None, 'fsdp'), may hold values from -6 to 6
- momentum: float32 [8, 4, 448, 4096], P('tensor', 'region', None, 'fsdp'), may hold values from -4 to 4
Outputs:
- new_params: bfloat16 [14336, 4096], P('tensor', 'fsdp')
The draws below stay inside these ranges and needn't reach their ends.
All inputs are finite; a program needn't handle non-finite values.
Results may differ from the reference program's by a relative error of at most 0.0017.
Values may be sent and summed in bfloat16 or wider, within the bound.
No kernel may reach another device: no remote copies, remote signals or barrier semaphores. Data moves between devices by JAX's collectives and lax.ppermute only.
A program may use at most 192 MiB of HBM per device.

```python
import math
import jax
import jax.numpy as jnp

D = 4096
FF = 14336
TOK_DEV = 512
TOK_R = 2048
N_REGION = 4
N_FSDP = 4
N_TENSOR = 8


def block_levels(stream_key, shape, shards, least, high):
    factor_of, own = 1.0, jax.random.fold_in(stream_key, 6)
    for position, shards_of in shards:
        steps = jnp.exp(jax.random.uniform(jax.random.fold_in(own, position), (shards_of,), jnp.float32, least / len(shards), high / len(shards)))
        factor_of = factor_of * jnp.repeat(steps, shape[position] // shards_of).reshape([-1 if axis == position else 1 for axis in range(len(shape))])
    return factor_of


def scatter_about(rng, shape, scale, bound, split=(), kind=jnp.bfloat16):
    result = jax.random.normal(rng, shape, jnp.float32) * scale
    if len(split) > 0:
        result = block_levels(rng, shape, split, -0.22, 0.18) * result
    return jnp.clip(result, min=-bound, max=bound).astype(kind)


def setup_inputs(seed: int = 0) -> dict:
    arg_keys = jax.random.split(jax.random.key(seed), 9)
    return {
        "gate_pre": scatter_about(arg_keys[0], (N_REGION, TOK_R, FF), 1.0, 6.0, ((0, 4), (1, 4), (2, 8))),
        "up_pre": scatter_about(arg_keys[1], (N_REGION, TOK_R, FF), 1.0, 6.0, ((0, 4), (1, 4), (2, 8))),
        "out_grad": scatter_about(arg_keys[2], (N_REGION, TOK_R, D), 1.0, 6.0, ((0, 4), (1, 8), (2, 4))),
        "weights": scatter_about(arg_keys[3], (N_REGION, FF, D), 1.0, 6.0, ((0, 4), (1, 8), (2, 4))),
        "first_moment": scatter_about(arg_keys[4], (N_REGION, FF, D), 0.001, 0.015625, ((0, 4), (1, 8), (2, 4))),
        "second_moment": jnp.clip(jnp.exp(math.log(9.999999747378752e-06) - 2.3025851 * jax.random.uniform(arg_keys[5], (N_REGION, FF, D), jnp.float32) ** block_levels(arg_keys[5], (N_REGION, FF, D), ((0, 4), (1, 8), (2, 4)), -0.2, 0.2)), 9.999999974752427e-07, 9.999999747378752e-06),
        "anchor": scatter_about(arg_keys[6], (N_TENSOR, N_REGION, FF // (N_TENSOR * N_REGION), D), 1.0, 6.0, ((0, 8), (1, 4), (3, 4)), jnp.float32),
        "momentum": scatter_about(arg_keys[7], (N_TENSOR, N_REGION, FF // (N_TENSOR * N_REGION), D), 0.3, 4.0, ((0, 8), (1, 4), (3, 4)), jnp.float32),
    }


decay_first = 0.9
decay_second = 0.95
inner_rate = 0.25
weight_decay = 0.1
epsilon = 1e-08
outer_rate = 0.7
nesterov = 0.9

def reference(gate_pre, up_pre, out_grad, weights, first_moment, second_moment, anchor, momentum):
    hidden = (jax.nn.silu(gate_pre.astype(jnp.float32)) * up_pre.astype(jnp.float32)).astype(jnp.bfloat16)
    running = jnp.zeros((FF, D), jnp.float32)
    for region in range(N_REGION):
        gradient = jnp.dot(hidden[region].T, out_grad[region], preferred_element_type=jnp.float32) * (1.0 / (TOK_DEV * N_FSDP))
        first_new = decay_first * first_moment[region].astype(jnp.float32) + (1.0 - decay_first) * gradient
        second_new = decay_second * second_moment[region] + (1.0 - decay_second) * gradient * gradient
        master = weights[region].astype(jnp.float32)
        inner = master - inner_rate * (first_new / (jnp.sqrt(second_new) + epsilon) + weight_decay * master)
        running = running + inner
    anchor_full = anchor.reshape(FF, D)
    momentum_full = momentum.reshape(FF, D)
    pseudo = anchor_full - running / N_REGION
    momentum_new = nesterov * momentum_full + pseudo
    return (anchor_full - outer_rate * (pseudo + nesterov * momentum_new)).astype(jnp.bfloat16)
```

```python
import functools

import jax
import jax.numpy as jnp
from jax import lax
from jax.experimental import pallas as pl
from jax.experimental.pallas import tpu as pltpu
from jax.sharding import PartitionSpec as P

decay_first = 0.9
decay_second = 0.95
inner_rate = 0.25
weight_decay = 0.1
epsilon = 1e-08
outer_rate = 0.7
nesterov = 0.9

SIZES = (128, 128, 128, 64)
OWNERS = 4
VMEM = 48 * 1024 * 1024


def offsets(sizes):
    return [sum(sizes[:i]) for i in range(len(sizes))]


def activate_kernel(gate_ref, up_ref, *chunk_refs):
    gate = gate_ref[...].astype(jnp.float32)
    up = up_ref[...].astype(jnp.float32)
    hidden = (gate / (1.0 + jnp.exp(-gate)) * up).astype(jnp.bfloat16)
    turned = hidden.T
    owned = turned.shape[0] // OWNERS
    start = 0
    for ref in chunk_refs:
        rows = ref.shape[0] // OWNERS
        for o in range(OWNERS):
            ref[o * rows : (o + 1) * rows, :] = turned[o * owned + start : o * owned + start + rows, :]
        start += rows


def activate(gate, up, sizes, block=128):
    tokens, units = gate.shape
    spec = pl.BlockSpec((block, units), lambda i: (i, 0))
    return pl.pallas_call(
        activate_kernel,
        grid=(tokens // block,),
        in_specs=[spec, spec],
        out_specs=[pl.BlockSpec((OWNERS * n, block), lambda i: (0, i)) for n in sizes],
        out_shape=[jax.ShapeDtypeStruct((OWNERS * n, tokens), jnp.bfloat16) for n in sizes],
        compiler_params=pltpu.CompilerParams(vmem_limit_bytes=VMEM),
        cost_estimate=pl.CostEstimate(
            flops=6 * tokens * units, bytes_accessed=6 * tokens * units, transcendentals=tokens * units
        ),
        name="activate",
    )(gate, up)


def inner_kernel(where, *refs):
    pieces, refs = refs[:8], refs[8:]
    own, before, after, far_a, far_b, weights, first, second, keep, send, grads, sems = refs
    d, steps = pl.program_id(0), pl.num_programs(0)
    z, y, x_lo, core = where[0], where[1], where[2], where[3]
    width = weights.shape[2]
    hops = (0, 0, 3, 3, 1, 1, 2, 2)

    def fetch(i, tile):
        block = lax.rem(y + hops[i], 4)
        half = x_lo if i % 2 == 0 else 1 - x_lo
        row = pl.multiple_of(block * 512 + half * 256, 256)
        cols = pl.ds(tile * width, width)
        return pltpu.make_async_copy(
            pieces[i].at[:, cols], grads.at[tile, pl.ds(row, 256), :], sems.at[tile, i]
        )

    tiles = grads.shape[0]

    @pl.when(d == 0)
    def _():
        for tile in range(tiles):
            for i in range(8):
                fetch(i, tile).start()

    for tile in range(tiles):

        @pl.when(d == tile)
        def _(tile=tile):
            for i in range(8):
                fetch(i, tile).wait()

    def block_of(hop):
        row = pl.multiple_of(lax.rem(z + hop, 4) * 512, 512)
        return grads[d, pl.ds(row, 512), :]

    def dot(a, b):
        return jnp.dot(a, b, preferred_element_type=jnp.float32)

    total = dot(own[...], block_of(0)) + dot(before[...], block_of(3)) + dot(after[...], block_of(1))
    far = block_of(2)
    total = total + jnp.concatenate([dot(far_a[...], far), dot(far_b[...], far)], axis=0)
    gradient = total * (1.0 / 2048)
    rows = weights.shape[1]
    gradient = gradient.reshape(OWNERS, rows, width)
    first_new = decay_first * first[...].astype(jnp.float32) + (1.0 - decay_first) * gradient
    second_new = decay_second * second[...] + (1.0 - decay_second) * gradient * gradient
    master = weights[...].astype(jnp.float32)
    inner = master - inner_rate * (first_new / (jnp.sqrt(second_new) + epsilon) + weight_decay * master)
    for c in range(2):

        @pl.when(core == c)
        def _(c=c):
            for h in range(2):
                keep[h] = inner[2 * h + c]
                send[h] = inner[2 * h + 1 - c]


def inner_step(where, pieces, hidden, weights, first, second, start, width=256):
    own, before, after, far_a, far_b = hidden
    rows = own.shape[0] // OWNERS
    columns = weights.shape[2]
    whole = lambda a: pl.BlockSpec(a.shape, lambda d, w: (0, 0))
    tile = pl.BlockSpec((OWNERS, rows, width), lambda d, w: (0, start // rows, d))
    out = pl.BlockSpec((2, rows, width), lambda d, w: (0, 0, d))
    shape = jax.ShapeDtypeStruct((2, rows, columns), jnp.float32)
    count = OWNERS * rows * columns
    return pl.pallas_call(
        inner_kernel,
        grid_spec=pltpu.PrefetchScalarGridSpec(
            num_scalar_prefetch=1,
            grid=(columns // width,),
            in_specs=[pl.BlockSpec(memory_space=pl.ANY)] * 8 + [whole(a) for a in hidden] + [tile] * 3,
            out_specs=[out, out],
            scratch_shapes=[
                pltpu.VMEM((columns // width, 2048, width), jnp.bfloat16),
                pltpu.SemaphoreType.DMA((columns // width, 8)),
            ],
        ),
        out_shape=[shape, shape],
        compiler_params=pltpu.CompilerParams(vmem_limit_bytes=VMEM),
        cost_estimate=pl.CostEstimate(
            flops=2 * 2048 * count, bytes_accessed=12 * count + 2 * 2048 * (columns + OWNERS * rows), transcendentals=count
        ),
        name="inner_step",
    )(where, *pieces, *hidden, weights, first, second)


def shift(x, axis, n, step):
    return lax.ppermute(x, axis, [(i, (i + step) % n) for i in range(n)])


def local(gate_pre, up_pre, out_grad, weights, first_moment, second_moment, anchor, momentum):
    z, t, r = lax.axis_index("fsdp"), lax.axis_index("tensor"), lax.axis_index("region")
    y, x_lo, half, core = t // 2, t % 2, r // 2, r % 2
    where = jnp.stack([z, y, x_lo, core]).astype(jnp.int32)
    along_z = functools.partial(shift, axis="fsdp", n=4)
    along_y = lambda x, step: shift(x, "tensor", 8, 2 * step)
    swap = lambda x, axis, n, bit: lax.ppermute(x, axis, [(i, i ^ bit) for i in range(n)])
    other_core = lambda x: swap(x, "region", 4, 1)
    other_chip = lambda x: swap(x, "region", 4, 2)

    mine = out_grad[0]
    pair = swap(mine, "tensor", 8, 1)
    mine_up, mine_down = along_y(mine, 1), along_y(mine, -1)
    pair_up, pair_down = along_y(pair, 1), along_y(pair, -1)
    mine_far, pair_far = along_y(mine_up, 1), along_y(pair_down, -1)
    pieces = [mine, pair, mine_up, pair_up, mine_down, pair_down, mine_far, pair_far]

    chunks = activate(gate_pre[0], up_pre[0], SIZES)
    gathered = []
    for own in chunks:
        before, after = along_z(own, step=1), along_z(own, step=-1)
        middle = own.shape[0] // 2
        far_a = along_z(before[:middle], step=1)
        far_b = along_z(after[middle:], step=-1)
        gathered.append((own, before, after, far_a, far_b))

    gain = outer_rate * (1.0 + nesterov)
    rest = (1.0 - gain) * anchor[0, 0] - outer_rate * nesterov * nesterov * momentum[0, 0]
    rest = rest.astype(jnp.float16)
    rest_there = other_chip(rest)
    rest = jnp.where(half == 0, jnp.stack([rest, rest_there]), jnp.stack([rest_there, rest]))

    by_owner = lambda a: a[0].reshape(OWNERS, 448, 1024)
    w, m, v = by_owner(weights), by_owner(first_moment), by_owner(second_moment)
    out = jnp.zeros((2, 2, 448, 1024), jnp.bfloat16)
    for hidden, rows, start in zip(gathered, SIZES, offsets(SIZES)):
        keep, send = inner_step(where, pieces, hidden, w, m, v, start)
        both = (keep + other_core(send)).astype(jnp.float16)
        both_there = other_chip(both)
        total = both.astype(jnp.float32) + both_there.astype(jnp.float32)
        fresh = rest[:, start : start + rows].astype(jnp.float32) + (gain / 4) * total
        fresh = fresh.astype(jnp.bfloat16)
        fresh_there = other_core(fresh)
        out = lax.dynamic_update_slice(out, fresh[:, None], (0, core, start, 0))
        out = lax.dynamic_update_slice(out, fresh_there[:, None], (0, 1 - core, start, 0))
    return out.reshape(1792, 1024)


def solution(mesh):
    placed = (
        P("region", "fsdp", "tensor"),
        P("region", "fsdp", "tensor"),
        P("region", "tensor", "fsdp"),
        P("region", "tensor", "fsdp"),
        P("region", "tensor", "fsdp"),
        P("region", "tensor", "fsdp"),
        P("tensor", "region", None, "fsdp"),
        P("tensor", "region", None, "fsdp"),
    )
    return jax.shard_map(
        local, mesh=mesh, in_specs=placed, out_specs=P("tensor", "fsdp"), check_vma=False
    )
```

```python
import functools

import jax
import jax.numpy as jnp
from jax import lax
from jax.experimental import pallas as pl
from jax.experimental.pallas import tpu as pltpu
from jax.sharding import PartitionSpec as P

decay_first = 0.9
decay_second = 0.95
inner_rate = 0.25
weight_decay = 0.1
epsilon = 1e-08
outer_rate = 0.7
nesterov = 0.9
gain = outer_rate * (1.0 + nesterov)

OWNERS, OWNED, TOKENS, WIDTH = 4, 448, 512, 1024
SIZES = (128, 128, 128, 64)
MIB = 1024 * 1024
COST_ACT, COST_PASS, COST_ASM, COST_INNER, COST_HOLD = (0, 0, 0, 0), {2: 0, 3: 8}, 30, 8, 16
VMEM, HBM = pltpu.VMEM, pltpu.HBM


def first_rows(k):
    begin = sum(SIZES[:k])
    return begin, (begin + 64 if k < len(SIZES) - 1 else 0)


def place_in_mesh():
    t, r = lax.axis_index("tensor"), lax.axis_index("region")
    return lax.axis_index("fsdp"), t // 2, lax.rem(t, 2), lax.rem(r, 2), r // 2


def put(x, space):
    return pltpu.with_memory_space_constraint(x, space)


def call(kernel, out, args, spaces, scratch, limit, name, after=(), aliases={}, cost=0):
    spaces = list(spaces) + [VMEM] * len(after)
    args = [put(a, s) for a, s in zip(list(args) + list(after), spaces)]
    skip = len(after)
    count = len(args) - skip

    def body(*refs):
        kernel(*refs[:count], *refs[count + skip :])

    leaves = out if isinstance(out, list) else [out]
    specs = [pl.BlockSpec(memory_space=o.memory_space) for o in leaves]
    return pl.pallas_call(
        body,
        in_specs=[pl.BlockSpec(memory_space=s) for s in spaces],
        out_specs=specs if isinstance(out, list) else specs[0],
        out_shape=out,
        scratch_shapes=scratch,
        input_output_aliases=aliases,
        compiler_params=pltpu.CompilerParams(vmem_limit_bytes=limit),
        cost_estimate=pl.CostEstimate(flops=1000 + int(cost * 1e9), bytes_accessed=1000, transcendentals=0),
        name=name,
    )(*args)


def activate(gate, up, k, passed=None, after=()):
    low, high = first_rows(k)
    if SIZES[k] == 128:
        lanes = [o * OWNED + (low, high)[o % 2] for o in range(OWNERS)]
    else:
        lanes = [h * 2 * OWNED + low for h in range(2)]
    count = len(lanes)
    rows = 128 * count
    half = OWNERS * SIZES[k - 2] // 2 if passed else 0

    def kernel(gate_ref, up_ref, *refs):
        outs, (gates, ups, sems) = refs[-5 if passed else -4 : -3], refs[-3:]
        copies = []
        for g, lane in enumerate(lanes):
            for s, (src, dst) in enumerate(((gate_ref, gates), (up_ref, ups))):
                copies.append(pltpu.make_async_copy(src.at[:, lane : lane + 128], dst.at[g], sems.at[g, s]))
        for copy in copies:
            copy.start()
        if passed:
            before, after = refs[:2]
            outs[0][rows:, :] = before[:half, :]
            outs[1][rows:, :] = after[half : 2 * half, :]
        for g in range(count):
            copies[2 * g].wait()
            copies[2 * g + 1].wait()
            gate = gates[g].astype(jnp.float32)
            hidden = (gate / (1.0 + jnp.exp(-gate)) * ups[g].astype(jnp.float32)).astype(jnp.bfloat16)
            turned = hidden.T
            for out in outs:
                out[128 * g : 128 * (g + 1), :] = turned

    block = VMEM((count, TOKENS, 128), jnp.bfloat16)
    out = VMEM((rows + half, TOKENS), jnp.bfloat16)
    return call(
        kernel,
        [out, out] if passed else out,
        [gate, up, *(passed or ())],
        [HBM, HBM] + [VMEM] * (2 if passed else 0),
        [block, block, pltpu.SemaphoreType.DMA((count, 2))],
        12 * MIB,
        f"activate{k}",
        after,
        cost=COST_ACT[k],
    )


def pass_on(passed, k):
    half = OWNERS * SIZES[k] // 2

    def kernel(before, after, up, down):
        up[...] = before[:half, :]
        down[...] = after[half : 2 * half, :]

    out = VMEM((half, TOKENS), jnp.bfloat16)
    return call(kernel, [out, out], passed, [VMEM] * 2, [], 4 * MIB, f"pass_on{k}", cost=COST_PASS[k])


def assemble(pieces):
    hops = (0, 0, 3, 3, 1, 1, 2, 2)

    def kernel(*refs):
        _, y, x_lo, _, _ = place_in_mesh()
        out_ref = refs[8]
        for i in range(8):
            part = x_lo if i % 2 == 0 else 1 - x_lo
            row = pl.multiple_of(lax.rem(y + hops[i], 4) * 512 + part * 256, 256)
            out_ref[pl.ds(row, 256), :] = refs[i][...]

    return call(
        kernel,
        VMEM((2048, WIDTH), jnp.bfloat16),
        pieces,
        [VMEM] * 8,
        [],
        8 * MIB,
        "assemble",
        cost=COST_ASM,
    )


def inner_step(grads, hidden, state, k, after=(), width=512):
    rows = SIZES[k]
    begins = first_rows(k)
    tiles = WIDTH // width
    scale = gain / 4
    step = scale * inner_rate

    def kernel(grads_ref, own, before, after, far_a, far_b, w, m, v, anchor, momentum, keep, send, *scratch):
        ws, ms, vs, anchors, momenta, sems = scratch
        z, _, _, core, half = place_in_mesh()
        mine = pl.multiple_of(begins[0] + core * (begins[1] - begins[0]), 16)
        copies = []
        for t in range(tiles):
            cols = pl.ds(t * width, width)
            group = []
            for s, (src, dst) in enumerate(((w, ws), (m, ms), (v, vs))):
                for o in range(OWNERS):
                    at = pl.ds(o * OWNED + begins[o % 2], rows)
                    group.append(pltpu.make_async_copy(src.at[at, cols], dst.at[t, o], sems.at[t, 4 * s + o]))
            for s, (src, dst) in enumerate(((anchor, anchors), (momentum, momenta))):
                group.append(pltpu.make_async_copy(src.at[pl.ds(mine, rows), cols], dst.at[t], sems.at[t, 12 + s]))
            copies.append(group)
        for group in copies:
            for copy in group:
                copy.start()

        count = OWNERS * rows

        def dot(a, hop, t, start=0, size=count):
            row = pl.multiple_of(lax.rem(z + hop, 4) * 512, 512)
            b = grads_ref[pl.ds(row, 512), t * width : (t + 1) * width]
            return jnp.dot(a[start : start + size, :], b, preferred_element_type=jnp.float32)

        for t in range(tiles):
            cols = slice(t * width, (t + 1) * width)
            total = dot(own, 0, t) + dot(before, 3, t) + dot(after, 1, t)
            fars = [dot(far, 2, t, far.shape[0] - count // 2, count // 2) for far in (far_a, far_b)]
            total = total + jnp.concatenate(fars, axis=0)
            total = total.reshape(OWNERS, rows, width)
            for copy in copies[t]:
                copy.wait()
            first_new = (step * decay_first) * ms[t].astype(jnp.float32) + (
                step * (1.0 - decay_first) / 2048
            ) * total
            second_new = decay_second * vs[t] + ((1.0 - decay_second) / 2048**2) * (total * total)
            root = second_new * lax.rsqrt(second_new)
            master = ws[t].astype(jnp.float32)
            inner = (scale * (1.0 - inner_rate * weight_decay)) * master - first_new / (root + epsilon)
            rest = (1.0 - gain) * anchors[t] - (outer_rate * nesterov * nesterov) * momenta[t]
            for o in range(OWNERS):

                @pl.when(core == o % 2)
                def _(o=o):
                    keep[o // 2, :, cols] = inner[o]

                @pl.when(core != o % 2)
                def _(o=o):
                    send[o // 2, :, cols] = inner[o]

            keep[half, :, cols] = keep[half, :, cols] + rest

    shape = VMEM((2, rows, WIDTH), jnp.float32)
    state_block = lambda dtype: VMEM((tiles, OWNERS, rows, width), dtype)
    owner_block = VMEM((tiles, rows, width), jnp.float32)
    return call(
        kernel,
        [shape, shape],
        [grads, *hidden, *state],
        [VMEM] * 6 + [HBM] * 5,
        [state_block(jnp.bfloat16), state_block(jnp.bfloat16), state_block(jnp.float32), owner_block, owner_block]
        + [pltpu.SemaphoreType.DMA((tiles, 14))],
        20 * MIB,
        f"inner{k}",
        after,
        cost=COST_INNER,
    )


def hold(arrays, k):
    def kernel(*refs):
        refs[-1][...] = jnp.zeros((8, 128), jnp.float32)

    return call(kernel, VMEM((8, 128), jnp.float32), arrays, [VMEM] * len(arrays), [], 4 * MIB, f"hold{k}", cost=COST_HOLD)


def place(mine, theirs, out, k):
    rows = SIZES[k]
    begins = first_rows(k)

    def kernel(mine_ref, theirs_ref, *refs):
        out_ref, sems = refs[-2:]
        core = place_in_mesh()[3]
        copies = []
        for i, src in enumerate((mine_ref, theirs_ref)):
            c = core if i == 0 else 1 - core
            row = pl.multiple_of(begins[0] + c * (begins[1] - begins[0]), 16)
            for h in range(2):
                copies.append(
                    pltpu.make_async_copy(src.at[h], out_ref.at[2 * h + c, pl.ds(row, rows), :], sems.at[i, h])
                )
        for copy in copies:
            copy.start()
        for copy in copies:
            copy.wait()

    before = [] if out is None else [out]
    return call(
        kernel,
        HBM((OWNERS, OWNED, WIDTH), jnp.bfloat16),
        [mine, theirs] + before,
        [VMEM, VMEM] + [HBM] * len(before),
        [pltpu.SemaphoreType.DMA((2, 2))],
        4 * MIB,
        f"place{k}",
        aliases={2: 0} if before else {},
    )


def shift(x, axis, n, step):
    return lax.ppermute(x, axis, [(i, (i + step) % n) for i in range(n)])


def local(gate_pre, up_pre, out_grad, weights, first_moment, second_moment, anchor, momentum):
    along_z = functools.partial(shift, axis="fsdp", n=4)
    along_y = lambda x, step: shift(x, "tensor", 8, 2 * step)
    swap = lambda x, axis, n, bit: lax.ppermute(x, axis, [(i, i ^ bit) for i in range(n)])
    other_core = lambda x: swap(x, "region", 4, 1)
    other_chip = lambda x: swap(x, "region", 4, 2)

    mine = out_grad[0]
    with jax.named_scope("pair"):
        pair = swap(mine, "tensor", 8, 1)
    with jax.named_scope("mine"):
        mine_up, mine_down = along_y(mine, 1), along_y(mine, -1)
    with jax.named_scope("paired"):
        pair_up, pair_down = along_y(pair, 1), along_y(pair, -1)
    with jax.named_scope("far"):
        mine_far, pair_far = along_y(mine_up, 1), along_y(pair_down, -1)
    grads = assemble([mine, pair, mine_up, pair_up, mine_down, pair_down, mine_far, pair_far])

    chunks = len(SIZES)
    owns, ring = [], []
    for k in range(chunks + 2):
        if k < 2:
            up = down = activate(gate_pre[0], up_pre[0], k)
        elif k < chunks:
            after = [owns[1], pair] if k == 2 else [mine_up, mine_down]
            up, down = activate(gate_pre[0], up_pre[0], k, ring[k - 2], after)
        else:
            up, down = pass_on(ring[k - 2], k - 2)
        owns.append(up)
        with jax.named_scope(f"ring{k}"):
            ring.append((along_z(up, step=1), along_z(down, step=-1)))
    gathered = [(owns[k], *ring[k], *ring[k + 2]) for k in range(chunks)]

    state = (weights[0], first_moment[0], second_moment[0], anchor[0, 0], momentum[0, 0])
    out, sums, results = None, [], []
    for k, hidden in enumerate(gathered):
        if k == 0:
            after = [owns[3], owns[4]]
        elif k == 1:
            after = [owns[5], sums[0]]
        else:
            after = [hold([*ring[k + 2], results[k - 2]], k), sums[k - 1]]
        keep, send = inner_step(grads, hidden, state, k, after)
        with jax.named_scope(f"cores{k}"):
            arrived = other_core(send)
        with jax.named_scope(f"sum{k}"):
            both = (keep + arrived).astype(jnp.float16)
            sums.append(both[0, :8, :128].astype(jnp.float32))
        with jax.named_scope(f"chips{k}"):
            both_there = other_chip(both)
        with jax.named_scope(f"fresh{k}"):
            results.append((both.astype(jnp.float32) + both_there.astype(jnp.float32)).astype(jnp.bfloat16))
    for k, fresh in enumerate(results):
        with jax.named_scope(f"share{k}"):
            shared = other_core(fresh)
        out = place(fresh, shared, out, k)
    return out.reshape(OWNERS * OWNED, WIDTH)


def solution(mesh):
    placed = (
        P("region", "fsdp", "tensor"),
        P("region", "fsdp", "tensor"),
        P("region", "tensor", "fsdp"),
        P("region", "tensor", "fsdp"),
        P("region", "tensor", "fsdp"),
        P("region", "tensor", "fsdp"),
        P("tensor", "region", None, "fsdp"),
        P("tensor", "region", None, "fsdp"),
    )
    return jax.shard_map(
        local, mesh=mesh, in_specs=placed, out_specs=P("tensor", "fsdp"), check_vma=False
    )
```

```python
import functools

import jax
import jax.numpy as jnp
from jax import lax
from jax.experimental import pallas as pl
from jax.experimental.pallas import tpu as pltpu
from jax.sharding import PartitionSpec as P

decay_first = 0.9
decay_second = 0.95
inner_rate = 0.25
weight_decay = 0.1
epsilon = 1e-08
outer_rate = 0.7
nesterov = 0.9
gain = outer_rate * (1.0 + nesterov)

OWNERS, OWNED, TOKENS, WIDTH = 4, 448, 512, 1024
SIZES = (176, 160, 112)
LOADED = (0, 1, 2)
MIB = 1024 * 1024
COST = dict(activate0=0, activate1=0, activate2=0, pass_on0=0, pass_on1=4, pass_on2=8, split=0, load0=8, load1=8, load2=4, assemble=0, inner0=0, inner1=0, inner2=0, hold1=0, gap0=0, gap1=0, gap2=8, gap3=0, place0=0, place1=0, place2=0)
VMEM, HBM = pltpu.VMEM, pltpu.HBM


def first_row(k):
    return sum(SIZES[:k])


def place_in_mesh():
    t, r = lax.axis_index("tensor"), lax.axis_index("region")
    return lax.axis_index("fsdp"), t // 2, lax.rem(t, 2), lax.rem(r, 2), r // 2


def put(x, space):
    return pltpu.with_memory_space_constraint(x, space)


def call(kernel, out, args, spaces, scratch, limit, name, after=(), aliases={}):
    spaces = list(spaces) + [VMEM] * len(after)
    args = [put(a, s) for a, s in zip(list(args) + list(after), spaces)]
    skip = len(after)
    count = len(args) - skip

    def body(*refs):
        kernel(*refs[:count], *refs[count + skip :])

    leaves = out if isinstance(out, list) else [out]
    specs = [pl.BlockSpec(memory_space=o.memory_space) for o in leaves]
    return pl.pallas_call(
        body,
        in_specs=[pl.BlockSpec(memory_space=s) for s in spaces],
        out_specs=specs if isinstance(out, list) else specs[0],
        out_shape=out,
        scratch_shapes=scratch,
        input_output_aliases=aliases,
        compiler_params=pltpu.CompilerParams(vmem_limit_bytes=limit),
        cost_estimate=pl.CostEstimate(flops=1000 + int(COST[name] * 1e9), bytes_accessed=1000, transcendentals=0),
        name=name,
    )(*args)


def activate(gate, up, chunks, after=()):
    size = sum(SIZES[k] for k in chunks)
    starts = [o * OWNED + first_row(chunks[0]) for o in range(OWNERS)]
    spans = [(start // 128 * 128, -(-(start + size) // 128) * 128) for start in starts]
    width = max(high - low for low, high in spans)

    def kernel(gate_ref, up_ref, *refs):
        outs, (gates, ups, sems) = refs[:-3], refs[-3:]
        copies = []
        for g, (low, high) in enumerate(spans):
            for s, (src, dst) in enumerate(((gate_ref, gates), (up_ref, ups))):
                copies.append(
                    pltpu.make_async_copy(src.at[:, low:high], dst.at[g, :, : high - low], sems.at[g, s])
                )
        for copy in copies:
            copy.start()
        for g, (low, high) in enumerate(spans):
            copies[2 * g].wait()
            copies[2 * g + 1].wait()
            gate = gates[g, :, : high - low].astype(jnp.float32)
            up = ups[g, :, : high - low].astype(jnp.float32)
            turned = (gate / (1.0 + jnp.exp(-gate)) * up).astype(jnp.bfloat16).T
            skip = starts[g] - low
            for k, out in zip(chunks, outs):
                out[g * SIZES[k] : (g + 1) * SIZES[k], :] = turned[skip : skip + SIZES[k], :]
                skip += SIZES[k]

    block = VMEM((OWNERS, TOKENS, width), jnp.bfloat16)
    return call(
        kernel,
        [VMEM((OWNERS * SIZES[k], TOKENS), jnp.bfloat16) for k in chunks],
        [gate, up],
        [HBM, HBM],
        [block, block, pltpu.SemaphoreType.DMA((OWNERS, 2))],
        16 * MIB,
        f"activate{chunks[0]}",
        after,
    )


def halves(first, second, name, after=()):
    half = first.shape[0] // 2

    def kernel(first_ref, second_ref, low, high):
        low[...] = first_ref[:half, :]
        high[...] = second_ref[half:, :]

    out = VMEM((half, first.shape[1]), jnp.bfloat16)
    return call(kernel, [out, out], [first, second], [VMEM] * 2, [], 4 * MIB, name, after)


def assemble(pieces, after=()):
    def kernel(*refs):
        _, y, x_lo, _, _ = place_in_mesh()
        out_ref = refs[-1]
        for ref, (_, hop, other, part) in zip(refs, pieces):
            rows = ref.shape[0]
            token = lax.rem(y + hop, 4) * 512 + (1 - x_lo if other else x_lo) * 256 + part * 128
            out_ref[pl.ds(pl.multiple_of(token, 128), rows), :] = ref[...]

    return call(
        kernel,
        VMEM((2048, WIDTH), jnp.bfloat16),
        [p[0] for p in pieces],
        [VMEM] * len(pieces),
        [],
        8 * MIB,
        "assemble",
        after,
    )


def state_blocks(k):
    rows = SIZES[k]
    block = lambda dtype: VMEM((OWNERS, rows, WIDTH), dtype)
    owned = VMEM((rows, WIDTH), jnp.float32)
    return [block(jnp.bfloat16), block(jnp.bfloat16), block(jnp.float32), owned, owned]


def state_copies(k, sources, targets, sems, cols, t):
    begin = first_row(k)
    rows = SIZES[k]
    copies = []
    for s in range(3):
        for o in range(OWNERS):
            at = pl.ds(o * OWNED + begin, rows)
            copies.append((sources[s].at[at, cols], targets[s].at[o, :, cols], sems.at[t, 4 * s + o]))
    for s in (3, 4):
        copies.append((sources[s].at[pl.ds(begin, rows), cols], targets[s].at[:, cols], sems.at[t, 9 + s]))
    return [pltpu.make_async_copy(*copy) for copy in copies]


def load(state, k, after=()):
    def kernel(*refs):
        copies = state_copies(k, refs[:5], refs[5:10], refs[10], slice(0, WIDTH), 0)
        for copy in copies:
            copy.start()
        for copy in copies:
            copy.wait()

    return call(
        kernel, state_blocks(k), state, [HBM] * 5, [pltpu.SemaphoreType.DMA((1, 14))], 4 * MIB, f"load{k}", after
    )


def inner_step(grads, hidden, state, loaded, k, after=(), width=512):
    rows = SIZES[k]
    tiles = WIDTH // width
    scale = gain / 4
    step = scale * inner_rate
    count = OWNERS * rows

    def kernel(grads_ref, own, before, after, far_a, far_b, *refs):
        z, _, _, core, half = place_in_mesh()
        keep, send = refs[5:7]
        copies = []
        if loaded:
            here = refs[:5]
        else:
            here, sems = refs[7:12], refs[12]
            for t in range(tiles):
                copies.append(state_copies(k, refs[:5], here, sems, pl.ds(t * width, width), t))
        ws, ms, vs, anchors, momenta = here
        for group in copies:
            for copy in group:
                copy.start()

        def dot(a, hop, cols, start=0, size=count):
            row = pl.multiple_of(lax.rem(z + hop, 4) * 512, 512)
            return jnp.dot(a[start : start + size, :], grads_ref[pl.ds(row, 512), cols], preferred_element_type=jnp.float32)

        for t in range(tiles):
            cols = slice(t * width, (t + 1) * width)
            total = dot(own, 0, cols) + dot(before, 3, cols) + dot(after, 1, cols)
            total = total + jnp.concatenate([dot(far, 2, cols, 0, count // 2) for far in (far_a, far_b)], axis=0)
            total = total.reshape(OWNERS, rows, width)
            for copy in copies[t] if copies else ():
                copy.wait()
            first_new = (step * decay_first) * ms[:, :, cols].astype(jnp.float32) + (
                step * (1.0 - decay_first) / 2048
            ) * total
            second_new = decay_second * vs[:, :, cols] + ((1.0 - decay_second) / 2048**2) * (total * total)
            root = second_new * lax.rsqrt(second_new)
            master = ws[:, :, cols].astype(jnp.float32)
            inner = (scale * (1.0 - inner_rate * weight_decay)) * master - first_new / (root + epsilon)
            rest = (1.0 - gain) * anchors[:, cols] - (outer_rate * nesterov * nesterov) * momenta[:, cols]
            for o in range(OWNERS):

                @pl.when(core == o % 2)
                def _(o=o):
                    keep[o // 2, :, cols] = inner[o]

                @pl.when(core != o % 2)
                def _(o=o):
                    send[o // 2, :, cols] = inner[o]

            keep[half, :, cols] = keep[half, :, cols] + rest

    shape = VMEM((2, rows, WIDTH), jnp.float32)
    return call(
        kernel,
        [shape, shape],
        [grads, *hidden, *state],
        [VMEM] * 6 + [VMEM if loaded else HBM] * 5,
        [] if loaded else [*state_blocks(k), pltpu.SemaphoreType.DMA((tiles, 14))],
        20 * MIB,
        f"inner{k}",
        after,
    )


def hold(arrays, k):
    def kernel(*refs):
        refs[-1][...] = jnp.zeros((8, 128), jnp.float32)

    return call(kernel, VMEM((8, 128), jnp.float32), arrays, [VMEM] * len(arrays), [], 4 * MIB, f"hold{k}")


def gap(array, name, after=()):
    out = VMEM(array.shape, array.dtype)
    return call(lambda a, b: None, out, [array], [VMEM], [], 4 * MIB, name, after, {0: 0})


def place(mine, theirs, out, k, after=()):
    rows = SIZES[k]
    begin = first_row(k)

    def kernel(mine_ref, theirs_ref, *refs):
        out_ref, said, sems = refs[-3:]
        core = place_in_mesh()[3]
        copies = []
        for i, src in enumerate((mine_ref, theirs_ref)):
            c = core if i == 0 else 1 - core
            for h in range(2):
                copies.append(
                    pltpu.make_async_copy(src.at[h], out_ref.at[2 * h + c, pl.ds(begin, rows), :], sems.at[i, h])
                )
        for copy in copies:
            copy.start()
        said[...] = jnp.zeros((8, 128), jnp.float32)
        for copy in copies:
            copy.wait()

    before = [] if out is None else [out]
    return call(
        kernel,
        [HBM((OWNERS, OWNED, WIDTH), jnp.bfloat16), VMEM((8, 128), jnp.float32)],
        [mine, theirs] + before,
        [VMEM, VMEM] + [HBM] * len(before),
        [pltpu.SemaphoreType.DMA((2, 2))],
        4 * MIB,
        f"place{k}",
        after,
        {2: 0} if before else {},
    )


def shift(x, axis, n, step):
    return lax.ppermute(x, axis, [(i, (i + step) % n) for i in range(n)])


def local(gate_pre, up_pre, out_grad, weights, first_moment, second_moment, anchor, momentum):
    along_z = functools.partial(shift, axis="fsdp", n=4)
    along_y = lambda x, step: shift(x, "tensor", 8, 2 * step)
    swap = lambda x, axis, n, bit: lax.ppermute(x, axis, [(i, i ^ bit) for i in range(n)])
    other_core = lambda x: swap(x, "region", 4, 1)
    other_chip = lambda x: swap(x, "region", 4, 2)

    state = (weights[0], first_moment[0], second_moment[0], anchor[0, 0], momentum[0, 0])
    gate, up = gate_pre[0], up_pre[0]

    def both_ways(up, down, name):
        with jax.named_scope(name):
            return along_z(up, step=1), along_z(down, step=-1)

    mine = out_grad[0]
    with jax.named_scope("pair"):
        pair = swap(mine, "tensor", 8, 1)
    with jax.named_scope("mine"):
        mine_up, mine_down = along_y(mine, 1), along_y(mine, -1)
    own = activate(gate, up, (0,))
    ring = {0: both_ways(own[0], own[0], "ring0")}
    with jax.named_scope("down"):
        pair_down = along_y(pair, -1)
    with jax.named_scope("cross"):
        cross_up = swap(mine_up, "tensor", 8, 1)
    with jax.named_scope("far"):
        mine_far = along_y(mine_up, 1)
    step = own[:1]
    loaded0 = load(state, 0, step)
    step = [loaded0[3]]
    on = halves(*ring[0], "pass_on0", [*step, pair, mine_up, mine_down])
    passed = {0: both_ways(*on, "on0")}
    last = halves(cross_up, pair_down, "split", [on[0], mine_far])
    with jax.named_scope("last"):
        last_up, last_down = along_y(last[0], 1), along_y(last[1], -1)
    own += activate(gate, up, (1,), last[:1])
    ring[1] = both_ways(own[1], own[1], "ring1")
    grads = assemble(
        [
            (mine, 0, False, 0),
            (pair, 0, True, 0),
            (mine_up, 3, False, 0),
            (cross_up, 3, True, 0),
            (mine_down, 1, False, 0),
            (pair_down, 1, True, 0),
            (mine_far, 2, False, 0),
            (last_up, 2, True, 0),
            (last_down, 2, True, 1),
        ],
    )

    out, sums, results, later, placed = None, [], [], [], []

    def finish(k, out, after=()):
        with jax.named_scope(f"share{k}"):
            shared = other_core(results[k])
        out, said = place(results[k], shared, out, k, after)
        placed.append(said)
        return out

    for k in range(len(SIZES)):
        after = []
        if k == 0:
            mine_state = loaded0
        else:
            previous = [sums[k - 1]]
            if k == 1:
                own += activate(gate, up, (2,), previous)
                ring[2] = both_ways(own[2], own[2], "ring2")
                previous = own[2:]
            mine_state = load(state, k, previous)
            if k == 1:
                after = [hold([*passed[k], mine_state[3]], k)]
        hidden = (own[k], *ring[k], *passed[k])
        keep, other = inner_step(grads, hidden, mine_state, True, k, after)
        if k + 1 < len(SIZES):
            on = halves(*ring[k + 1], f"pass_on{k + 1}", [keep, *results[:k]])
            passed[k + 1] = both_ways(*on, f"on{k + 1}")
            waited = [on[0]]
        else:
            out = finish(0, out)
            waited = placed
        with jax.named_scope(f"cores{k}"):
            arrived = other_core(other.astype(jnp.float16)).astype(jnp.float32)
        with jax.named_scope(f"sum{k}"):
            later.append(gap(keep, f"gap{k}", waited))
            both = (later[k] + arrived).astype(jnp.float16)
            sums.append(both[0, :8, :128].astype(jnp.float32))
        with jax.named_scope(f"chips{k}"):
            both_there = other_chip(both)
        with jax.named_scope(f"fresh{k}"):
            results.append((both.astype(jnp.float32) + both_there.astype(jnp.float32)).astype(jnp.bfloat16))
    out = finish(1, out)
    results[2] = gap(results[2], "gap3", placed[1:])
    out = finish(2, out)
    return out.reshape(OWNERS * OWNED, WIDTH)


def solution(mesh):
    placed = (
        P("region", "fsdp", "tensor"),
        P("region", "fsdp", "tensor"),
        P("region", "tensor", "fsdp"),
        P("region", "tensor", "fsdp"),
        P("region", "tensor", "fsdp"),
        P("region", "tensor", "fsdp"),
        P("tensor", "region", None, "fsdp"),
        P("tensor", "region", None, "fsdp"),
    )
    return jax.shard_map(
        local, mesh=mesh, in_specs=placed, out_specs=P("tensor", "fsdp"), check_vma=False
    )
```

```python
import functools

import jax
import jax.numpy as jnp
from jax import lax
from jax.experimental import pallas as pl
from jax.experimental.pallas import tpu as pltpu
from jax.sharding import PartitionSpec as P

decay_first = 0.9
decay_second = 0.95
inner_rate = 0.25
weight_decay = 0.1
epsilon = 1e-08
outer_rate = 0.7
nesterov = 0.9
gain = outer_rate * (1.0 + nesterov)

OWNERS, OWNED, TOKENS, WIDTH = 4, 448, 512, 1024
SIZES = (176, 160, 112)
LOADED = (0, 1, 2)
MIB = 1024 * 1024
COST = dict(near1=0, near2=8, activate0=0, activate1=0, gap_ring1=0, gap_ring2=0, tick=4, pass_on0=0, pass_on1=1, pass_on2=8, split=0, load0=8, load1=0, load2=4, assemble=0, inner0=0, inner1=0, inner2=0, hold1=0, gap0=0, gap1=0, gap2=8, gap3=0, place0=0, place1=0, place2=0)
VMEM, HBM = pltpu.VMEM, pltpu.HBM


def first_row(k):
    return sum(SIZES[:k])


def place_in_mesh():
    t, r = lax.axis_index("tensor"), lax.axis_index("region")
    return lax.axis_index("fsdp"), t // 2, lax.rem(t, 2), lax.rem(r, 2), r // 2


def put(x, space):
    return pltpu.with_memory_space_constraint(x, space)


def call(kernel, out, args, spaces, scratch, limit, name, after=(), aliases={}):
    spaces = list(spaces) + [VMEM] * len(after)
    args = [put(a, s) for a, s in zip(list(args) + list(after), spaces)]
    skip = len(after)
    count = len(args) - skip

    def body(*refs):
        kernel(*refs[:count], *refs[count + skip :])

    leaves = out if isinstance(out, list) else [out]
    specs = [pl.BlockSpec(memory_space=o.memory_space) for o in leaves]
    return pl.pallas_call(
        body,
        in_specs=[pl.BlockSpec(memory_space=s) for s in spaces],
        out_specs=specs if isinstance(out, list) else specs[0],
        out_shape=out,
        scratch_shapes=scratch,
        input_output_aliases=aliases,
        compiler_params=pltpu.CompilerParams(vmem_limit_bytes=limit),
        cost_estimate=pl.CostEstimate(flops=1000 + int(COST[name] * 1e9), bytes_accessed=1000, transcendentals=0),
        name=name,
    )(*args)


def activate(gate, up, chunks, after=()):
    size = sum(SIZES[k] for k in chunks)
    starts = [o * OWNED + first_row(chunks[0]) for o in range(OWNERS)]
    spans = [(start // 128 * 128, -(-(start + size) // 128) * 128) for start in starts]
    width = max(high - low for low, high in spans)

    def kernel(gate_ref, up_ref, *refs):
        outs, (gates, ups, sems) = refs[:-3], refs[-3:]
        copies = []
        for g, (low, high) in enumerate(spans):
            for s, (src, dst) in enumerate(((gate_ref, gates), (up_ref, ups))):
                copies.append(
                    pltpu.make_async_copy(src.at[:, low:high], dst.at[g, :, : high - low], sems.at[g, s])
                )
        for copy in copies:
            copy.start()
        for g, (low, high) in enumerate(spans):
            copies[2 * g].wait()
            copies[2 * g + 1].wait()
            gate = gates[g, :, : high - low].astype(jnp.float32)
            up = ups[g, :, : high - low].astype(jnp.float32)
            turned = (gate / (1.0 + jnp.exp(-gate)) * up).astype(jnp.bfloat16).T
            skip = starts[g] - low
            for k, out in zip(chunks, outs):
                out[g * SIZES[k] : (g + 1) * SIZES[k], :] = turned[skip : skip + SIZES[k], :]
                skip += SIZES[k]

    block = VMEM((OWNERS, TOKENS, width), jnp.bfloat16)
    return call(
        kernel,
        [VMEM((OWNERS * SIZES[k], TOKENS), jnp.bfloat16) for k in chunks],
        [gate, up],
        [HBM, HBM],
        [block, block, pltpu.SemaphoreType.DMA((OWNERS, 2))],
        16 * MIB,
        f"activate{chunks[0]}",
        after,
    )


def halves(first, second, name, after=()):
    half = first.shape[0] // 2

    def kernel(first_ref, second_ref, low, high):
        low[...] = first_ref[:half, :]
        high[...] = second_ref[half:, :]

    out = VMEM((half, first.shape[1]), jnp.bfloat16)
    return call(kernel, [out, out], [first, second], [VMEM] * 2, [], 4 * MIB, name, after)


def assemble(pieces, after=()):
    def kernel(*refs):
        _, y, x_lo, _, _ = place_in_mesh()
        out_ref = refs[-1]
        for ref, (_, hop, other, part) in zip(refs, pieces):
            rows = ref.shape[0]
            token = lax.rem(y + hop, 4) * 512 + (1 - x_lo if other else x_lo) * 256 + part * 128
            out_ref[pl.ds(pl.multiple_of(token, 128), rows), :] = ref[...]

    return call(
        kernel,
        VMEM((2048, WIDTH), jnp.bfloat16),
        [p[0] for p in pieces],
        [VMEM] * len(pieces),
        [],
        8 * MIB,
        "assemble",
        after,
    )


def state_blocks(k):
    rows = SIZES[k]
    block = lambda dtype: VMEM((OWNERS, rows, WIDTH), dtype)
    owned = VMEM((rows, WIDTH), jnp.float32)
    return [block(jnp.bfloat16), block(jnp.bfloat16), block(jnp.float32), owned, owned]


def state_copies(k, sources, targets, sems, cols, t):
    begin = first_row(k)
    rows = SIZES[k]
    copies = []
    for s in range(3):
        for o in range(OWNERS):
            at = pl.ds(o * OWNED + begin, rows)
            copies.append((sources[s].at[at, cols], targets[s].at[o, :, cols], sems.at[t, 4 * s + o]))
    for s in (3, 4):
        copies.append((sources[s].at[pl.ds(begin, rows), cols], targets[s].at[:, cols], sems.at[t, 9 + s]))
    return [pltpu.make_async_copy(*copy) for copy in copies]


def load(state, k, after=()):
    def kernel(*refs):
        copies = state_copies(k, refs[:5], refs[5:10], refs[10], slice(0, WIDTH), 0)
        for copy in copies:
            copy.start()
        for copy in copies:
            copy.wait()

    return call(
        kernel, state_blocks(k), state, [HBM] * 5, [pltpu.SemaphoreType.DMA((1, 14))], 4 * MIB, f"load{k}", after
    )


def near_step(grads, hidden, k, after=(), width=512):
    count = OWNERS * SIZES[k]

    def kernel(grads_ref, own, before, after, total):
        z = place_in_mesh()[0]
        for t in range(WIDTH // width):
            cols = slice(t * width, (t + 1) * width)
            parts = []
            for ref, hop in ((own, 0), (before, 3), (after, 1)):
                row = pl.multiple_of(lax.rem(z + hop, 4) * 512, 512)
                parts.append(jnp.dot(ref[...], grads_ref[pl.ds(row, 512), cols], preferred_element_type=jnp.float32))
            total[:, cols] = parts[0] + parts[1] + parts[2]

    out = VMEM((count, WIDTH), jnp.float32)
    return call(kernel, out, [grads, *hidden], [VMEM] * 4, [], 12 * MIB, f"near{k}", after)


def inner_step(grads, hidden, state, loaded, k, after=(), width=512):
    rows = SIZES[k]
    tiles = WIDTH // width
    scale = gain / 4
    step = scale * inner_rate
    count = OWNERS * rows

    near = len(hidden) == 3

    def kernel(grads_ref, *refs):
        hidden_refs, refs = refs[: len(hidden)], refs[len(hidden) :]
        far_a, far_b = hidden_refs[-2:]
        z, _, _, core, half = place_in_mesh()
        keep, send = refs[5:7]
        copies = []
        if loaded:
            here = refs[:5]
        else:
            here, sems = refs[7:12], refs[12]
            for t in range(tiles):
                copies.append(state_copies(k, refs[:5], here, sems, pl.ds(t * width, width), t))
        ws, ms, vs, anchors, momenta = here
        for group in copies:
            for copy in group:
                copy.start()

        def dot(a, hop, cols, start=0, size=count):
            row = pl.multiple_of(lax.rem(z + hop, 4) * 512, 512)
            return jnp.dot(a[start : start + size, :], grads_ref[pl.ds(row, 512), cols], preferred_element_type=jnp.float32)

        for t in range(tiles):
            cols = slice(t * width, (t + 1) * width)
            if near:
                total = hidden_refs[0][:, cols]
            else:
                own, before, after = hidden_refs[:3]
                total = dot(own, 0, cols) + dot(before, 3, cols) + dot(after, 1, cols)
            total = total + jnp.concatenate([dot(far, 2, cols, 0, count // 2) for far in (far_a, far_b)], axis=0)
            total = total.reshape(OWNERS, rows, width)
            for copy in copies[t] if copies else ():
                copy.wait()
            first_new = (step * decay_first) * ms[:, :, cols].astype(jnp.float32) + (
                step * (1.0 - decay_first) / 2048
            ) * total
            second_new = decay_second * vs[:, :, cols] + ((1.0 - decay_second) / 2048**2) * (total * total)
            root = second_new * lax.rsqrt(second_new)
            master = ws[:, :, cols].astype(jnp.float32)
            inner = (scale * (1.0 - inner_rate * weight_decay)) * master - first_new / (root + epsilon)
            rest = (1.0 - gain) * anchors[:, cols] - (outer_rate * nesterov * nesterov) * momenta[:, cols]
            for o in range(OWNERS):

                @pl.when(core == o % 2)
                def _(o=o):
                    keep[o // 2, :, cols] = inner[o]

                @pl.when(core != o % 2)
                def _(o=o):
                    send[o // 2, :, cols] = inner[o]

            keep[half, :, cols] = keep[half, :, cols] + rest

    shape = VMEM((2, rows, WIDTH), jnp.float32)
    return call(
        kernel,
        [shape, shape],
        [grads, *hidden, *state],
        [VMEM] * (1 + len(hidden)) + [VMEM if loaded else HBM] * 5,
        [] if loaded else [*state_blocks(k), pltpu.SemaphoreType.DMA((tiles, 14))],
        20 * MIB,
        f"inner{k}",
        after,
    )


def hold(arrays, name):
    def kernel(*refs):
        refs[-1][...] = jnp.zeros((8, 128), jnp.float32)

    return call(kernel, VMEM((8, 128), jnp.float32), arrays, [VMEM] * len(arrays), [], 4 * MIB, name)


def gap(array, name, after=()):
    out = VMEM(array.shape, array.dtype)
    return call(lambda a, b: None, out, [array], [VMEM], [], 4 * MIB, name, after, {0: 0})


def place(pieces, out, name):
    count = len(pieces)

    def kernel(*refs):
        out_ref, said, sems = refs[-3:]
        core = place_in_mesh()[3]
        copies = []
        for i, (ref, (_, theirs, k)) in enumerate(zip(refs, pieces)):
            c = 1 - core if theirs else core
            for h in range(2):
                to = out_ref.at[2 * h + c, pl.ds(first_row(k), SIZES[k]), :]
                copies.append(pltpu.make_async_copy(ref.at[h], to, sems.at[i, h]))
        for copy in copies:
            copy.start()
        said[...] = jnp.zeros((8, 128), jnp.float32)
        for copy in copies:
            copy.wait()

    before = [] if out is None else [out]
    return call(
        kernel,
        [HBM((OWNERS, OWNED, WIDTH), jnp.bfloat16), VMEM((8, 128), jnp.float32)],
        [p[0] for p in pieces] + before,
        [VMEM] * count + [HBM] * len(before),
        [pltpu.SemaphoreType.DMA((count, 2))],
        4 * MIB,
        name,
        aliases={count: 0} if before else {},
    )


def shift(x, axis, n, step):
    return lax.ppermute(x, axis, [(i, (i + step) % n) for i in range(n)])


def local(gate_pre, up_pre, out_grad, weights, first_moment, second_moment, anchor, momentum):
    along_z = functools.partial(shift, axis="fsdp", n=4)
    along_y = lambda x, step: shift(x, "tensor", 8, 2 * step)
    swap = lambda x, axis, n, bit: lax.ppermute(x, axis, [(i, i ^ bit) for i in range(n)])
    other_core = lambda x: swap(x, "region", 4, 1)
    other_chip = lambda x: swap(x, "region", 4, 2)

    state = (weights[0], first_moment[0], second_moment[0], anchor[0, 0], momentum[0, 0])
    gate, up = gate_pre[0], up_pre[0]

    def both_ways(up, down, name):
        with jax.named_scope(name):
            return along_z(up, step=1), along_z(down, step=-1)

    mine = out_grad[0]
    with jax.named_scope("pair"):
        pair = swap(mine, "tensor", 8, 1)
    with jax.named_scope("mine"):
        mine_up, mine_down = along_y(mine, 1), along_y(mine, -1)
    own = list(activate(gate, up, (0,)))
    later_own = activate(gate, up, (1, 2), own)
    ring = {0: both_ways(own[0], own[0], "ring0")}
    with jax.named_scope("down"):
        pair_down = along_y(pair, -1)
    with jax.named_scope("cross"):
        cross_up = swap(mine_up, "tensor", 8, 1)
    with jax.named_scope("far"):
        mine_far = along_y(mine_up, 1)
    loaded = [load(state, 0, later_own[:1])]
    loaded.append(load(state, 1, loaded[0][3:4]))
    on = halves(*ring[0], "pass_on0", [loaded[1][3], pair, mine_up, mine_down])
    passed = {0: both_ways(*on, "on0")}
    last = halves(cross_up, pair_down, "split", [on[0], mine_far])
    with jax.named_scope("last"):
        last_up, last_down = along_y(last[0], 1), along_y(last[1], -1)
    own.append(gap(later_own[0], "gap_ring1", last[:1]))
    ring[1] = both_ways(own[1], own[1], "ring1")
    grads = assemble(
        [
            (mine, 0, False, 0),
            (pair, 0, True, 0),
            (mine_up, 3, False, 0),
            (cross_up, 3, True, 0),
            (mine_down, 1, False, 0),
            (pair_down, 1, True, 0),
            (mine_far, 2, False, 0),
            (last_up, 2, True, 0),
            (last_down, 2, True, 1),
        ],
    )

    sums, results, later = [], [], []

    def share(k):
        with jax.named_scope(f"share{k}"):
            return other_core(results[k])

    for k in range(len(SIZES)):
        after = []
        if k == 1:
            own.append(gap(later_own[1], "gap_ring2", sums))
            ring[2] = both_ways(own[2], own[2], "ring2")
            near = near_step(grads, (own[1], *ring[1]), 1, own[2:])
            after = [hold([*passed[k], hold([near], "tick")], "hold1")]
        if k == 2:
            loaded.append(load(state, 2, sums[1:]))
            near = near_step(grads, (own[2], *ring[2]), 2, loaded[2][3:4])
        hidden = (near, *passed[k]) if k else (own[k], *ring[k], *passed[k])
        keep, other = inner_step(grads, hidden, loaded[k], True, k, after)
        if k + 1 < len(SIZES):
            on = halves(*ring[k + 1], f"pass_on{k + 1}", [keep, *results[:k]])
            passed[k + 1] = both_ways(*on, f"on{k + 1}")
            waited = [on[0]]
        else:
            results[0] = gap(results[0], "gap3", loaded[2][3:4])
            out, said = place([(results[0], False, 0), (share(0), True, 0)], None, "place0")
            waited = [said]
        with jax.named_scope(f"cores{k}"):
            arrived = other_core(other.astype(jnp.float16)).astype(jnp.float32)
        with jax.named_scope(f"sum{k}"):
            later.append(gap(keep, f"gap{k}", waited))
            both = (later[k] + arrived).astype(jnp.float16)
            sums.append(both[0, :8, :128].astype(jnp.float32))
        with jax.named_scope(f"chips{k}"):
            both_there = other_chip(both)
        with jax.named_scope(f"fresh{k}"):
            results.append((both.astype(jnp.float32) + both_there.astype(jnp.float32)).astype(jnp.bfloat16))
    out, _ = place([(results[1], False, 1), (share(1), True, 1), (results[2], False, 2)], out, "place1")
    out, _ = place([(share(2), True, 2)], out, "place2")
    return out.reshape(OWNERS * OWNED, WIDTH)


def solution(mesh):
    placed = (
        P("region", "fsdp", "tensor"),
        P("region", "fsdp", "tensor"),
        P("region", "tensor", "fsdp"),
        P("region", "tensor", "fsdp"),
        P("region", "tensor", "fsdp"),
        P("region", "tensor", "fsdp"),
        P("tensor", "region", None, "fsdp"),
        P("tensor", "region", None, "fsdp"),
    )
    return jax.shard_map(
        local, mesh=mesh, in_specs=placed, out_specs=P("tensor", "fsdp"), check_vma=False
    )
```

```python
import functools

import jax
import jax.numpy as jnp
from jax import lax
from jax.experimental import pallas as pl
from jax.experimental.pallas import tpu as pltpu
from jax.sharding import PartitionSpec as P

decay_first = 0.9
decay_second = 0.95
inner_rate = 0.25
weight_decay = 0.1
epsilon = 1e-08
outer_rate = 0.7
nesterov = 0.9
gain = outer_rate * (1.0 + nesterov)

OWNERS, OWNED, TOKENS, WIDTH = 4, 448, 512, 1024
SIZES = (176, 160, 112)
LOADED = (0, 1, 2)
MIB = 1024 * 1024
COST = dict(near1=0, near2=8, activate0=0, activate1=0, gap_ring1=0, gap_ring2=0, tick=4, pass_on0=0, pass_on1=1, pass_on2=8, split=0, load0=8, load1=0, load2=4, assemble=0, inner0=0, inner1=0, inner2=0, hold1=0, gap0=0, gap1=0, gap2=8, gap3=0, place0=0, place1=0, place2=0)
VMEM, HBM = pltpu.VMEM, pltpu.HBM


def first_row(k):
    return sum(SIZES[:k])


def place_in_mesh():
    t, r = lax.axis_index("tensor"), lax.axis_index("region")
    return lax.axis_index("fsdp"), t // 2, lax.rem(t, 2), lax.rem(r, 2), r // 2


def put(x, space):
    return pltpu.with_memory_space_constraint(x, space)


def call(kernel, out, args, spaces, scratch, limit, name, after=(), aliases={}):
    spaces = list(spaces) + [VMEM] * len(after)
    args = [put(a, s) for a, s in zip(list(args) + list(after), spaces)]
    skip = len(after)
    count = len(args) - skip

    def body(*refs):
        kernel(*refs[:count], *refs[count + skip :])

    leaves = out if isinstance(out, list) else [out]
    specs = [pl.BlockSpec(memory_space=o.memory_space) for o in leaves]
    return pl.pallas_call(
        body,
        in_specs=[pl.BlockSpec(memory_space=s) for s in spaces],
        out_specs=specs if isinstance(out, list) else specs[0],
        out_shape=out,
        scratch_shapes=scratch,
        input_output_aliases=aliases,
        compiler_params=pltpu.CompilerParams(vmem_limit_bytes=limit),
        cost_estimate=pl.CostEstimate(flops=1000 + int(COST[name] * 1e9), bytes_accessed=1000, transcendentals=0),
        name=name,
    )(*args)


def activate(gate, up, chunks, after=()):
    size = sum(SIZES[k] for k in chunks)
    starts = [o * OWNED + first_row(chunks[0]) for o in range(OWNERS)]
    spans = [(start // 128 * 128, -(-(start + size) // 128) * 128) for start in starts]
    width = max(high - low for low, high in spans)

    part = TOKENS // 2

    def kernel(gate_ref, up_ref, *refs):
        outs, (gates, ups, sems) = refs[:-3], refs[-3:]
        steps = []
        for g, (low, high) in enumerate(spans):
            for t in range(2):
                rows = pl.ds(t * part, part)
                pair = [
                    pltpu.make_async_copy(src.at[rows, low:high], dst.at[g, rows, : high - low], sems.at[g, t, s])
                    for s, (src, dst) in enumerate(((gate_ref, gates), (up_ref, ups)))
                ]
                steps.append((g, t, pair))
        for _, _, pair in steps:
            for copy in pair:
                copy.start()
        for g, t, pair in steps:
            for copy in pair:
                copy.wait()
            low, high = spans[g]
            rows = slice(t * part, (t + 1) * part)
            gate = gates[g, rows, : high - low].astype(jnp.float32)
            up = ups[g, rows, : high - low].astype(jnp.float32)
            turned = (gate / (1.0 + jnp.exp(-gate)) * up).astype(jnp.bfloat16).T
            skip = starts[g] - low
            for k, out in zip(chunks, outs):
                out[g * SIZES[k] : (g + 1) * SIZES[k], rows] = turned[skip : skip + SIZES[k], :]
                skip += SIZES[k]

    block = VMEM((OWNERS, TOKENS, width), jnp.bfloat16)
    return call(
        kernel,
        [VMEM((OWNERS * SIZES[k], TOKENS), jnp.bfloat16) for k in chunks],
        [gate, up],
        [HBM, HBM],
        [block, block, pltpu.SemaphoreType.DMA((OWNERS, 2, 2))],
        16 * MIB,
        f"activate{chunks[0]}",
        after,
    )


def halves(first, second, name, after=()):
    half = first.shape[0] // 2

    def kernel(first_ref, second_ref, low, high):
        low[...] = first_ref[:half, :]
        high[...] = second_ref[half:, :]

    out = VMEM((half, first.shape[1]), jnp.bfloat16)
    return call(kernel, [out, out], [first, second], [VMEM] * 2, [], 4 * MIB, name, after)


def assemble(pieces, after=()):
    def kernel(*refs):
        _, y, x_lo, _, _ = place_in_mesh()
        out_ref = refs[-1]
        for ref, (_, hop, other, part) in zip(refs, pieces):
            rows = ref.shape[0]
            token = lax.rem(y + hop, 4) * 512 + (1 - x_lo if other else x_lo) * 256 + part * 128
            out_ref[pl.ds(pl.multiple_of(token, 128), rows), :] = ref[...]

    return call(
        kernel,
        VMEM((2048, WIDTH), jnp.bfloat16),
        [p[0] for p in pieces],
        [VMEM] * len(pieces),
        [],
        8 * MIB,
        "assemble",
        after,
    )


def state_blocks(k):
    rows = SIZES[k]
    block = lambda dtype: VMEM((OWNERS, rows, WIDTH), dtype)
    owned = VMEM((rows, WIDTH), jnp.float32)
    return [block(jnp.bfloat16), block(jnp.bfloat16), block(jnp.float32), owned, owned]


def state_copies(k, sources, targets, sems, cols, t):
    begin = first_row(k)
    rows = SIZES[k]
    copies = []
    for s in range(3):
        for o in range(OWNERS):
            at = pl.ds(o * OWNED + begin, rows)
            copies.append((sources[s].at[at, cols], targets[s].at[o, :, cols], sems.at[t, 4 * s + o]))
    for s in (3, 4):
        copies.append((sources[s].at[pl.ds(begin, rows), cols], targets[s].at[:, cols], sems.at[t, 9 + s]))
    return [pltpu.make_async_copy(*copy) for copy in copies]


def load(state, k, after=()):
    def kernel(*refs):
        copies = state_copies(k, refs[:5], refs[5:10], refs[10], slice(0, WIDTH), 0)
        for copy in copies:
            copy.start()
        for copy in copies:
            copy.wait()

    return call(
        kernel, state_blocks(k), state, [HBM] * 5, [pltpu.SemaphoreType.DMA((1, 14))], 4 * MIB, f"load{k}", after
    )


def near_step(grads, hidden, k, after=(), width=512):
    count = OWNERS * SIZES[k]

    def kernel(grads_ref, own, before, after, total):
        z = place_in_mesh()[0]
        for t in range(WIDTH // width):
            cols = slice(t * width, (t + 1) * width)
            parts = []
            for ref, hop in ((own, 0), (before, 3), (after, 1)):
                row = pl.multiple_of(lax.rem(z + hop, 4) * 512, 512)
                parts.append(jnp.dot(ref[...], grads_ref[pl.ds(row, 512), cols], preferred_element_type=jnp.float32))
            total[:, cols] = parts[0] + parts[1] + parts[2]

    out = VMEM((count, WIDTH), jnp.float32)
    return call(kernel, out, [grads, *hidden], [VMEM] * 4, [], 12 * MIB, f"near{k}", after)


def inner_step(grads, hidden, state, loaded, k, after=(), width=512):
    rows = SIZES[k]
    tiles = WIDTH // width
    scale = gain / 4
    step = scale * inner_rate
    count = OWNERS * rows

    near = len(hidden) == 3

    def kernel(grads_ref, *refs):
        hidden_refs, refs = refs[: len(hidden)], refs[len(hidden) :]
        far_a, far_b = hidden_refs[-2:]
        z, _, _, core, half = place_in_mesh()
        keep, send = refs[5:7]
        copies = []
        if loaded:
            here = refs[:5]
        else:
            here, sems = refs[7:12], refs[12]
            for t in range(tiles):
                copies.append(state_copies(k, refs[:5], here, sems, pl.ds(t * width, width), t))
        ws, ms, vs, anchors, momenta = here
        for group in copies:
            for copy in group:
                copy.start()

        def dot(a, hop, cols, start=0, size=count):
            row = pl.multiple_of(lax.rem(z + hop, 4) * 512, 512)
            return jnp.dot(a[start : start + size, :], grads_ref[pl.ds(row, 512), cols], preferred_element_type=jnp.float32)

        for t in range(tiles):
            cols = slice(t * width, (t + 1) * width)
            if near:
                total = hidden_refs[0][:, cols]
            else:
                own, before, after = hidden_refs[:3]
                total = dot(own, 0, cols) + dot(before, 3, cols) + dot(after, 1, cols)
            total = total + jnp.concatenate([dot(far, 2, cols, 0, count // 2) for far in (far_a, far_b)], axis=0)
            total = total.reshape(OWNERS, rows, width)
            for copy in copies[t] if copies else ():
                copy.wait()
            first_new = (step * decay_first) * ms[:, :, cols].astype(jnp.float32) + (
                step * (1.0 - decay_first) / 2048
            ) * total
            second_new = decay_second * vs[:, :, cols] + ((1.0 - decay_second) / 2048**2) * (total * total)
            root = second_new * lax.rsqrt(second_new)
            master = ws[:, :, cols].astype(jnp.float32)
            inner = (scale * (1.0 - inner_rate * weight_decay)) * master - first_new / (root + epsilon)
            rest = (1.0 - gain) * anchors[:, cols] - (outer_rate * nesterov * nesterov) * momenta[:, cols]
            for o in range(OWNERS):

                @pl.when(core == o % 2)
                def _(o=o):
                    keep[o // 2, :, cols] = inner[o]

                @pl.when(core != o % 2)
                def _(o=o):
                    send[o // 2, :, cols] = inner[o]

            keep[half, :, cols] = keep[half, :, cols] + rest

    shape = VMEM((2, rows, WIDTH), jnp.float32)
    return call(
        kernel,
        [shape, shape],
        [grads, *hidden, *state],
        [VMEM] * (1 + len(hidden)) + [VMEM if loaded else HBM] * 5,
        [] if loaded else [*state_blocks(k), pltpu.SemaphoreType.DMA((tiles, 14))],
        20 * MIB,
        f"inner{k}",
        after,
    )


def hold(arrays, name):
    def kernel(*refs):
        refs[-1][...] = jnp.zeros((8, 128), jnp.float32)

    return call(kernel, VMEM((8, 128), jnp.float32), arrays, [VMEM] * len(arrays), [], 4 * MIB, name)


def gap(array, name, after=()):
    out = VMEM(array.shape, array.dtype)
    return call(lambda a, b: None, out, [array], [VMEM], [], 4 * MIB, name, after, {0: 0})


def place(pieces, out, name):
    count = len(pieces)

    def kernel(*refs):
        out_ref, said, sems = refs[-3:]
        core = place_in_mesh()[3]
        copies = []
        for i, (ref, (_, theirs, k)) in enumerate(zip(refs, pieces)):
            c = 1 - core if theirs else core
            for h in range(2):
                to = out_ref.at[2 * h + c, pl.ds(first_row(k), SIZES[k]), :]
                copies.append(pltpu.make_async_copy(ref.at[h], to, sems.at[i, h]))
        for copy in copies:
            copy.start()
        said[...] = jnp.zeros((8, 128), jnp.float32)
        for copy in copies:
            copy.wait()

    before = [] if out is None else [out]
    return call(
        kernel,
        [HBM((OWNERS, OWNED, WIDTH), jnp.bfloat16), VMEM((8, 128), jnp.float32)],
        [p[0] for p in pieces] + before,
        [VMEM] * count + [HBM] * len(before),
        [pltpu.SemaphoreType.DMA((count, 2))],
        4 * MIB,
        name,
        aliases={count: 0} if before else {},
    )


def shift(x, axis, n, step):
    return lax.ppermute(x, axis, [(i, (i + step) % n) for i in range(n)])


def local(gate_pre, up_pre, out_grad, weights, first_moment, second_moment, anchor, momentum):
    along_z = functools.partial(shift, axis="fsdp", n=4)
    along_y = lambda x, step: shift(x, "tensor", 8, 2 * step)
    swap = lambda x, axis, n, bit: lax.ppermute(x, axis, [(i, i ^ bit) for i in range(n)])
    other_core = lambda x: swap(x, "region", 4, 1)
    other_chip = lambda x: swap(x, "region", 4, 2)

    state = (weights[0], first_moment[0], second_moment[0], anchor[0, 0], momentum[0, 0])
    gate, up = gate_pre[0], up_pre[0]

    def both_ways(up, down, name):
        with jax.named_scope(name):
            return along_z(up, step=1), along_z(down, step=-1)

    mine = out_grad[0]
    with jax.named_scope("pair"):
        pair = swap(mine, "tensor", 8, 1)
    with jax.named_scope("mine"):
        mine_up, mine_down = along_y(mine, 1), along_y(mine, -1)
    own = list(activate(gate, up, (0,)))
    later_own = activate(gate, up, (1, 2), own)
    ring = {0: both_ways(own[0], own[0], "ring0")}
    with jax.named_scope("down"):
        pair_down = along_y(pair, -1)
    with jax.named_scope("cross"):
        cross_up = swap(mine_up, "tensor", 8, 1)
    with jax.named_scope("far"):
        mine_far = along_y(mine_up, 1)
    loaded = [load(state, 0, later_own[:1])]
    loaded.append(load(state, 1, loaded[0][3:4]))
    on = halves(*ring[0], "pass_on0", [loaded[1][3], pair, mine_up, mine_down])
    passed = {0: both_ways(*on, "on0")}
    last = halves(cross_up, pair_down, "split", [on[0], mine_far])
    with jax.named_scope("last"):
        last_up, last_down = along_y(last[0], 1), along_y(last[1], -1)
    own.append(gap(later_own[0], "gap_ring1", last[:1]))
    ring[1] = both_ways(own[1], own[1], "ring1")
    grads = assemble(
        [
            (mine, 0, False, 0),
            (pair, 0, True, 0),
            (mine_up, 3, False, 0),
            (cross_up, 3, True, 0),
            (mine_down, 1, False, 0),
            (pair_down, 1, True, 0),
            (mine_far, 2, False, 0),
            (last_up, 2, True, 0),
            (last_down, 2, True, 1),
        ],
    )

    sums, results, later = [], [], []

    def share(k):
        with jax.named_scope(f"share{k}"):
            return other_core(results[k])

    for k in range(len(SIZES)):
        after = []
        if k == 1:
            own.append(gap(later_own[1], "gap_ring2", sums))
            ring[2] = both_ways(own[2], own[2], "ring2")
            near = near_step(grads, (own[1], *ring[1]), 1, own[2:])
            after = [hold([*passed[k], hold([near], "tick")], "hold1")]
        if k == 2:
            loaded.append(load(state, 2, sums[1:]))
            near = near_step(grads, (own[2], *ring[2]), 2, loaded[2][3:4])
        hidden = (near, *passed[k]) if k else (own[k], *ring[k], *passed[k])
        keep, other = inner_step(grads, hidden, loaded[k], True, k, after)
        if k + 1 < len(SIZES):
            on = halves(*ring[k + 1], f"pass_on{k + 1}", [keep, *results[:k]])
            passed[k + 1] = both_ways(*on, f"on{k + 1}")
            waited = [on[0]]
        else:
            results[0] = gap(results[0], "gap3", loaded[2][3:4])
            out, said = place([(results[0], False, 0), (share(0), True, 0)], None, "place0")
            waited = [said]
        with jax.named_scope(f"cores{k}"):
            arrived = other_core(other.astype(jnp.float16)).astype(jnp.float32)
        with jax.named_scope(f"sum{k}"):
            later.append(gap(keep, f"gap{k}", waited))
            both = (later[k] + arrived).astype(jnp.float16)
            sums.append(both[0, :8, :128].astype(jnp.float32))
        with jax.named_scope(f"chips{k}"):
            both_there = other_chip(both)
        with jax.named_scope(f"fresh{k}"):
            results.append((both.astype(jnp.float32) + both_there.astype(jnp.float32)).astype(jnp.bfloat16))
    out, _ = place([(results[1], False, 1), (share(1), True, 1), (results[2], False, 2)], out, "place1")
    out, _ = place([(share(2), True, 2)], out, "place2")
    return out.reshape(OWNERS * OWNED, WIDTH)


def solution(mesh):
    placed = (
        P("region", "fsdp", "tensor"),
        P("region", "fsdp", "tensor"),
        P("region", "tensor", "fsdp"),
        P("region", "tensor", "fsdp"),
        P("region", "tensor", "fsdp"),
        P("region", "tensor", "fsdp"),
        P("tensor", "region", None, "fsdp"),
        P("tensor", "region", None, "fsdp"),
    )
    return jax.shard_map(
        local, mesh=mesh, in_specs=placed, out_specs=P("tensor", "fsdp"), check_vma=False
    )
```
